1024 devices in a mesh: gx: 4 (over z_lo), gy: 16 (over z_hi, y), gz: 16 (over x, core).
Axes of the slice: x: 8, y: 8, z: 8 (z_hi: 2, z_lo: 4; z = z_hi * 4 + z_lo), core: 2. Of those that a mesh axis runs over, the one named last changes fastest.
Arguments:
- solution: float32 [56, 9, 131072], P(None, None, ('gx', 'gy', 'gz')), may hold values from -6 to 6
- jacobians: float32 [3, 9, 9, 131072], P(None, None, None, ('gx', 'gy', 'gz')), may hold values from -2 to 2
- derivative_stiffness: float32 [3, 56, 56], replicated, may hold values from -0.75 to 0.75
- volume_stiffness: float32 [3, 56, 56], replicated, may hold values from -0.375 to 0.375
- face_project: float32 [4, 21, 56], replicated, may hold values from -0.75 to 0.75
- face_lift: float32 [4, 56, 21], replicated, may hold values from -0.625 to 0.625
- face_rotation: float32 [3, 21, 21], replicated, may hold values from -1.25 to 1.25
- local_solver: float32 [4, 9, 9, 131072], P(None, None, None, ('gx', 'gy', 'gz')), may hold values from -2 to 2
- neighbour_solver: float32 [4, 9, 9, 131072], P(None, None, None, ('gx', 'gy', 'gz')), may hold values from -2 to 2
- cluster: int32 [131072], P(('gx', 'gy', 'gz')), may hold values from 0 to 2
- neighbours: int32 [4, 131072], P(None, ('gx', 'gy', 'gz')), may hold values from 0 to 1279, as said below
- orient: int32 [4, 131072], P(None, ('gx', 'gy', 'gz')), may hold values from 0 to 2
- send_faces: int32 [6, 131072], P(None, ('gx', 'gy', 'gz')), may hold values from 0 to 511
- counts: int32 [6, 1024], P(None, ('gx', 'gy', 'gz')), may hold values from 64 to 128, as said below
Outputs:
- advanced: float32 [56, 9, 131072], P(None, None, ('gx', 'gy', 'gz'))
The draws below stay inside these ranges and needn't reach their ends.
Inputs may be any that keep to these rules, and one draw needn't show every extreme that they name: `neighbours`: below 512 a value names a face of the own partition; above, a slot of the blocks of one direction whose index is below the sending partition's count for that list. `send_faces`: each value is a local face j * 128 + n of the sending partition. `counts`: entry [k, p] is how many leading slots of partition p's list k are used; some entry equals 128.
All inputs are finite; a program needn't handle non-finite values.
Results may differ from the reference program's by a relative error of at most 0.0001.
Values sent between devices are 32-bit elements; how exact they have to be, the bound alone decides.
A program may use at most 64 MiB of HBM per device.

```python
import math
import jax
import jax.numpy as jnp
from jax import lax

E_DEV = 128
SLOTS = 128
BASIS = 56
QUANTITIES = 9
FACE_BASIS = 21
DERIVATIVES = 6
SUBSTEPS = 4
ELEMENTS = 131072
N_GX = 4
N_GY = 16
N_GZ = 16
DEVICES = 1024


def block_counts(key):
    base_key = jax.random.fold_in(key, 7)
    lowest_count = (SLOTS + 1) // 2
    drawn = jax.random.randint(jax.random.fold_in(base_key, 1), (6 * DEVICES,), lowest_count, SLOTS + 1)
    chosen_entry = jax.random.randint(jax.random.fold_in(base_key, 2), (), 0, 6 * DEVICES)
    drawn = jnp.where(jnp.arange(6 * DEVICES, dtype=jnp.int32) == chosen_entry, SLOTS, drawn)
    return drawn.reshape(6, DEVICES).astype(jnp.int32)


def draw_counts(key, part):
    return block_counts(key)


def draw_neighbours(key, part):
    grid_counts = block_counts(key).reshape(6, N_GX, N_GY, N_GZ)
    received = jnp.stack([jnp.roll(grid_counts[0], 1, 0), jnp.roll(grid_counts[1], -1, 0), jnp.roll(grid_counts[2], 1, 1), jnp.roll(grid_counts[3], -1, 1), jnp.roll(grid_counts[4], 1, 2), jnp.roll(grid_counts[5], -1, 2)]).reshape(6, DEVICES)
    element_total = E_DEV * DEVICES
    owner_device = jnp.arange(element_total, dtype=jnp.int32) // E_DEV
    own_key = jax.random.fold_in(key, 9)
    inner_face = jax.random.randint(jax.random.fold_in(own_key, 1), (4, element_total), 0, 4 * E_DEV)
    direction = jax.random.randint(jax.random.fold_in(own_key, 2), (4, element_total), 0, 6)
    limit = received[direction, jnp.broadcast_to(owner_device[None, :], (4, element_total))]
    slot_index = jax.random.randint(jax.random.fold_in(own_key, 3), (4, element_total), 0, limit)
    is_ghost = jax.random.randint(jax.random.fold_in(own_key, 4), (4, element_total), 0, 4) == 0
    ghost_value = 4 * E_DEV + direction * SLOTS + slot_index
    return jnp.where(is_ghost, ghost_value, inner_face).astype(jnp.int32)


def with_ends(values, key, low, top_value):
    shape = values.shape
    place = [jax.random.randint(jax.random.fold_in(key, axis), (), 0, shape[axis]) for axis in range(len(shape))]
    values = values.at[tuple(place)].set(low)
    longest = shape.index(max(shape))
    place[longest] = (place[longest] + 1) % shape[longest]
    return values.at[tuple(place)].set(top_value)


def level_of(stream_key, extent, split, least, largest):
    def one(axis_at, shards_of):
        draws = jax.random.uniform(jax.random.fold_in(jax.random.fold_in(stream_key, 6), axis_at), (shards_of,), jnp.float32, least / len(split), largest / len(split))
        return jnp.repeat(jnp.exp(draws), extent[axis_at] // shards_of).reshape((-1,) + (1,) * (len(extent) - axis_at - 1))

    level = one(*split[0])
    for cut in split[1:]:
        level = level * one(*cut)
    return level


def gaussian(key, dims, spread, most, split=(), held_as=jnp.bfloat16):
    level = level_of(key, dims, split, -0.22, 0.18) if split else 1.0
    values = jax.random.normal(key, dims, jnp.float32) * spread * level
    return jnp.minimum(jnp.maximum(values, -most), most).astype(held_as)


def setup_inputs(seed: int = 0) -> dict:
    key_of = jax.random.split(jax.random.key(seed), 15)
    return {
        "solution": gaussian(key_of[0], (BASIS, QUANTITIES, ELEMENTS), 1.0, 6.0, ((2, 1024),), jnp.float32),
        "jacobians": gaussian(key_of[1], (3, QUANTITIES, QUANTITIES, ELEMENTS), 7 ** -0.5, 2.0, ((3, 1024),), jnp.float32),
        "derivative_stiffness": gaussian(key_of[2], (3, BASIS, BASIS), BASIS ** -0.5, 0.75, (), jnp.float32),
        "volume_stiffness": gaussian(key_of[3], (3, BASIS, BASIS), (4 * BASIS) ** -0.5, 0.375, (), jnp.float32),
        "face_project": gaussian(key_of[4], (4, FACE_BASIS, BASIS), BASIS ** -0.5, 0.75, (), jnp.float32),
        "face_lift": gaussian(key_of[5], (4, BASIS, FACE_BASIS), (4 * FACE_BASIS) ** -0.5, 0.625, (), jnp.float32),
        "face_rotation": gaussian(key_of[6], (3, FACE_BASIS, FACE_BASIS), FACE_BASIS ** -0.5, 1.25, (), jnp.float32),
        "local_solver": gaussian(key_of[7], (4, QUANTITIES, QUANTITIES, ELEMENTS), QUANTITIES ** -0.5, 2.0, ((3, 1024),), jnp.float32),
        "neighbour_solver": gaussian(key_of[8], (4, QUANTITIES, QUANTITIES, ELEMENTS), QUANTITIES ** -0.5, 2.0, ((3, 1024),), jnp.float32),
        "cluster": with_ends(jax.random.randint(key_of[9], (ELEMENTS,), 0, 3), jax.random.fold_in(key_of[9], 1), 0, 2).astype(jnp.int32),
        "neighbours": draw_neighbours(jax.random.fold_in(key_of[14], 71), 0),
        "orient": with_ends(jax.random.randint(key_of[11], (4, ELEMENTS), 0, 3), jax.random.fold_in(key_of[11], 1), 0, 2).astype(jnp.int32),
        "send_faces": with_ends(jax.random.randint(key_of[12], (6, SLOTS * DEVICES), 0, 4 * E_DEV), jax.random.fold_in(key_of[12], 1), 0, (4 * E_DEV) - 1).astype(jnp.int32),
        "counts": draw_counts(jax.random.fold_in(key_of[14], 71), 0),
    }


highest = lax.Precision.HIGHEST
coarse_span = 1.0


def derivative_terms(solution, jacobians, stiff_stack):
    current = solution
    results = [solution]
    for power_index in range(DERIVATIVES - 1):
        mixed_terms = jnp.dot(stiff_stack, current.reshape(BASIS, -1), precision=highest).reshape(3, BASIS, QUANTITIES, -1)
        current = -jnp.einsum("dkqe,dqpe->kpe", mixed_terms, jacobians, precision=highest)
        results.append(current)
    return results


def time_weights(cluster, substep):
    period = jnp.left_shift(jnp.ones_like(cluster), cluster)
    offset = (substep % period).astype(jnp.float32)
    finish = ((substep + 1) % period) == 0
    substep_span = coarse_span / SUBSTEPS
    upper_time = (offset + 1.0) * substep_span
    lower_time = offset * substep_span
    weight_rows = [(upper_time ** (power_index + 1) - lower_time ** (power_index + 1)) / math.factorial(power_index + 1) for power_index in range(DERIVATIVES)]
    return jnp.stack(weight_rows), finish


def volume_term(accumulated, jacobians, volume_stack):
    mixed_terms = jnp.dot(volume_stack, accumulated.reshape(BASIS, -1), precision=highest).reshape(3, BASIS, QUANTITIES, -1)
    return jnp.einsum("dkqe,dqpe->kpe", mixed_terms, jacobians, precision=highest)


def reference(solution, jacobians, derivative_stiffness, volume_stiffness, face_project, face_lift, face_rotation, local_solver, neighbour_solver, cluster, neighbours, orient, send_faces, counts):
    device_total = N_GX * N_GY * N_GZ
    face_count = 4 * E_DEV
    element_total = device_total * E_DEV
    block_width = FACE_BASIS * QUANTITIES
    owner_device = jnp.arange(element_total, dtype=jnp.int32) // E_DEV
    coordinates = [owner_device // (N_GY * N_GZ), (owner_device // N_GZ) % N_GY, owner_device % N_GZ]
    axis_sizes = [N_GX, N_GY, N_GZ]
    is_ghost = neighbours >= face_count
    remainder = jnp.maximum(neighbours - face_count, 0)
    direction = remainder // SLOTS
    slot_index = remainder % SLOTS
    axis_id = direction // 2
    shift_sign = jnp.where(direction % 2 == 0, -1, 1).astype(jnp.int32)
    inside_mesh = jnp.ones(neighbours.shape, dtype=bool)
    moved = []
    for axis_number in range(3):
        placed = coordinates[axis_number][None, :] + jnp.where(axis_id == axis_number, shift_sign, 0)
        inside_mesh = inside_mesh & (placed >= 0) & (placed < axis_sizes[axis_number])
        moved.append(jnp.clip(placed, 0, axis_sizes[axis_number] - 1))
    sender = ((moved[0] * N_GY + moved[1]) * N_GZ + moved[2]).astype(jnp.int32)
    face_id = send_faces.reshape(-1)[direction * (device_total * SLOTS) + sender * SLOTS + slot_index]
    slot_alive = slot_index < counts.reshape(-1)[direction * device_total + sender]
    zero_column = device_total * face_count
    remote_index = jnp.where(inside_mesh & slot_alive, sender * face_count + face_id, zero_column)
    global_index = jnp.where(is_ghost, remote_index, owner_device[None, :] * face_count + neighbours).astype(jnp.int32)

    stiff_stack = derivative_stiffness.reshape(3 * BASIS, BASIS)
    volume_stack = volume_stiffness.reshape(3 * BASIS, BASIS)
    project_stack = face_project.reshape(4 * FACE_BASIS, BASIS)
    rotation_stack = face_rotation.reshape(3 * FACE_BASIS, FACE_BASIS)
    lift_join = face_lift.transpose(1, 0, 2).reshape(BASIS, 4 * FACE_BASIS)
    orient_picks = (orient.reshape(-1)[None, :] == jnp.arange(3, dtype=jnp.int32)[:, None]).astype(jnp.float32)

    own_total = jnp.zeros_like(solution)
    flux_total = jnp.zeros_like(solution)
    for substep in range(SUBSTEPS):
        weights, finish = time_weights(cluster, substep)
        derivatives = derivative_terms(solution, jacobians, stiff_stack)
        integral = weights[0][None, None, :] * derivatives[0]
        for power_index in range(1, DERIVATIVES):
            integral = integral + weights[power_index][None, None, :] * derivatives[power_index]
        projected = jnp.dot(project_stack, integral.reshape(BASIS, -1), precision=highest).reshape(4, FACE_BASIS, QUANTITIES, element_total)
        face_table = projected.reshape(4, block_width, device_total, E_DEV).transpose(1, 2, 0, 3).reshape(block_width, device_total * face_count)
        face_table = jnp.concatenate([face_table, jnp.zeros((block_width, 1), jnp.float32)], axis=1)
        gathered = jnp.take(face_table, global_index.reshape(-1), axis=1)
        rotated = jnp.dot(rotation_stack, gathered.reshape(FACE_BASIS, -1), precision=highest).reshape(3, FACE_BASIS, QUANTITIES, 4 * element_total)
        chosen = jnp.einsum("hfqx,hx->fqx", rotated, orient_picks, precision=highest).reshape(FACE_BASIS, QUANTITIES, 4, element_total)
        neighbour_part = jnp.einsum("fqie,iqpe->ifpe", chosen, neighbour_solver, precision=highest)
        local_part = jnp.einsum("ifqe,iqpe->ifpe", projected, local_solver, precision=highest)
        flux_step = jnp.dot(lift_join, (local_part + neighbour_part).reshape(4 * FACE_BASIS, -1), precision=highest).reshape(BASIS, QUANTITIES, element_total)
        own_total = own_total + integral
        flux_total = flux_total + flux_step
        updated = solution + volume_term(own_total, jacobians, volume_stack) - flux_total
        ending = finish[None, None, :]
        solution = jnp.where(ending, updated, solution)
        own_total = jnp.where(ending, 0.0, own_total)
        flux_total = jnp.where(ending, 0.0, flux_total)
    return solution
```

```python
import jax
import jax.numpy as jnp
from jax import lax
from jax.experimental import pallas as pl
from jax.experimental.pallas import tpu as pltpu
from jax.sharding import PartitionSpec as P

BASIS = 56
QUANTITIES = 9
FACE_BASIS = 21
DERIVATIVES = 6
SUBSTEPS = 4
LANES = 128
FACES = 4
DIRECTIONS = 6
FACE_ROWS = 24
PACKED = 192
MESH = pl.DeviceIdType.MESH
AXES = ("gx", "gy", "gz")

f32 = jnp.float32
bf16 = jnp.bfloat16


def halves(value):
    high = value.astype(bf16).astype(f32)
    return high, value - high


def stacked(value):
    high, low = halves(value)
    return jnp.concatenate([high, low, high], axis=0).astype(bf16)


def place(rows, columns, offsets):
    row = lax.broadcasted_iota(jnp.int32, (rows, columns), 0)
    column = lax.broadcasted_iota(jnp.int32, (rows, columns), 1)
    hit = column == row + offsets[0]
    for offset in offsets[1:]:
        hit = hit | (column == row + offset)
    return jnp.where(hit, 1.0, 0.0).astype(bf16)


def widened(matrix, columns, first, second, third):
    high, low = halves(matrix)
    depth = matrix.shape[1]
    return jnp.dot(
        high.astype(bf16), place(depth, columns, (first, second)), preferred_element_type=f32
    ) + jnp.dot(low.astype(bf16), place(depth, columns, (third,)), preferred_element_type=f32)


def dot(left, right):
    return jnp.dot(left, right, preferred_element_type=f32)


def kernel(
    sol_ref, jac_ref, ds_ref, vs_ref, fp_ref, fl_ref, fr_ref, ls_ref, ns_ref,
    cluster_ref, neigh_ref, orient_ref, faces_ref, counts_ref, out_ref,
    cur, own, flux, integ, mixed, volume, operand, projected, table, pair,
    inner, total, chosen, zface, zstack, jac_b, ls_b, ns_b, weights,
    d_mat, v_mat, p_mat, l_mat, r_mat, build, build2, send_hot, recv_hot,
    send_buf, recv_buf, send_sem, recv_sem,
):
    index = [lax.axis_index(name) for name in AXES]
    count = [lax.axis_size(name) for name in AXES]
    has_lower = [index[a] > 0 for a in range(3)]
    has_higher = [index[a] < count[a] - 1 for a in range(3)]

    barrier = pltpu.get_barrier_semaphore()
    arrivals = jnp.int32(0)
    for a in range(3):
        for there, step in ((has_lower[a], -1), (has_higher[a], 1)):
            arrivals = arrivals + there.astype(jnp.int32)

            @pl.when(there)
            def _(a=a, step=step):
                pl.semaphore_signal(
                    barrier, inc=1, device_id={AXES[a]: index[a] + step}, device_id_type=MESH
                )

    for d in range(3):
        for q in range(QUANTITIES):
            for p in range(QUANTITIES):
                jac_b[(d * 9 + q) * 9 + p] = jnp.broadcast_to(jac_ref[d, q, p : p + 1, :], (8, LANES))
    d_mat[...] = widened(-ds_ref[...].reshape(3 * BASIS, BASIS), 3 * BASIS, 0, BASIS, 2 * BASIS).astype(bf16)
    for q in range(QUANTITIES):
        cur[q] = sol_ref[:, q, :]
        own[q] = jnp.zeros((BASIS, LANES), f32)
        flux[q] = jnp.zeros((BASIS, LANES), f32)
    build[...] = jnp.zeros_like(build)
    for j in range(FACES):
        build[j * FACE_ROWS : j * FACE_ROWS + FACE_BASIS, :] = widened(
            fp_ref[j], 3 * BASIS, 0, BASIS, 2 * BASIS
        )
    p_mat[...] = build[...].astype(bf16)
    slot = lax.broadcasted_iota(jnp.int32, (1, LANES), 1)
    face_row = lax.broadcasted_iota(jnp.int32, (FACES * LANES, LANES), 0)
    for k in range(DIRECTIONS):
        named = jnp.where(slot < counts_ref[k : k + 1, :], faces_ref[k : k + 1, :], -1)
        send_hot[:, k * LANES : (k + 1) * LANES] = jnp.where(face_row == named, 1.0, 0.0).astype(bf16)
    for a in range(3):
        for s in range(2):

            @pl.when(jnp.logical_not((has_lower, has_higher)[s][a]))
            def _(k=2 * a + s):
                for step in range(SUBSTEPS):
                    recv_buf[step, k] = jnp.zeros((PACKED, LANES), f32)

    def late_constants():
        block_row = lax.broadcasted_iota(jnp.int32, ((FACES + DIRECTIONS) * LANES, LANES), 0)
        for i in range(FACES):
            recv_hot[:, i * LANES : (i + 1) * LANES] = jnp.where(
                block_row == neigh_ref[i : i + 1, :], 1.0, 0.0
            ).astype(bf16)
        for i in range(FACES):
            for q in range(QUANTITIES):
                for p in range(QUANTITIES):
                    at = (i * 9 + q) * 9 + p
                    ls_b[at] = jnp.broadcast_to(ls_ref[i, q, p : p + 1, :], (8, LANES))
                    ns_b[at] = jnp.broadcast_to(ns_ref[i, q, p : p + 1, :], (8, LANES))
        v_mat[...] = widened(vs_ref[...].reshape(3 * BASIS, BASIS), 3 * BASIS, 0, BASIS, 2 * BASIS).astype(bf16)
        width = FACES * FACE_ROWS
        joined = jnp.zeros((BASIS, 3 * width), f32)
        for i in range(FACES):
            at = i * FACE_ROWS
            joined = joined + widened(fl_ref[i], 3 * width, at, width + at, 2 * width + at)
        l_mat[...] = joined.astype(bf16)
        build2[...] = jnp.zeros_like(build2)
        for o in range(3):
            build2[o * FACE_ROWS : o * FACE_ROWS + FACE_BASIS, :] = widened(
                fr_ref[o], 3 * FACE_ROWS, 0, FACE_ROWS, 2 * FACE_ROWS
            )
        r_mat[...] = build2[...].astype(bf16)

    late_constants()

    def columns(q, width=1):
        return slice(q * LANES, (q + width) * LANES)

    def mix(matrix):
        left = matrix[...]
        for q in range(0, QUANTITIES, 2):
            width = min(2, QUANTITIES - q)
            product = dot(left, operand[:, columns(q, width)])
            for w in range(width):
                mixed[q + w] = product[:, columns(w)]

    def apply_jacobians(sink):
        for p0 in range(0, QUANTITIES, 3):
            sums = [None] * 3
            for d in range(3):
                for q in range(QUANTITIES):
                    part = mixed[q, d * BASIS : (d + 1) * BASIS, :].reshape(7, 8, LANES)
                    for w in range(3):
                        term = part * jac_b[(d * 9 + q) * 9 + p0 + w][None]
                        sums[w] = term if sums[w] is None else sums[w] + term
            for w in range(3):
                sink(p0 + w, sums[w].reshape(BASIS, LANES))

    def copy(s, k):
        a, side = k // 2, k % 2
        return pltpu.make_async_remote_copy(
            src_ref=send_buf.at[s, k],
            dst_ref=recv_buf.at[s, k],
            send_sem=send_sem.at[s, k],
            recv_sem=recv_sem.at[s, k],
            device_id={AXES[a]: index[a] + (1, -1)[side]},
            device_id_type=MESH,
        )

    def sends(k):
        return (has_higher, has_lower)[k % 2][k // 2]

    def receives(k):
        return (has_lower, has_higher)[k % 2][k // 2]

    period = jnp.left_shift(jnp.ones((8, LANES), jnp.int32), jnp.broadcast_to(cluster_ref[...], (8, LANES)))

    def substep(s, carry):
        offset_int = s & (period - 1)
        ending = ((s + 1) & (period - 1)) == 0
        offset = offset_int.astype(f32)
        upper, lower = (offset + 1.0) * 0.25, offset * 0.25
        up, low, factorial = upper, lower, 1.0
        for m in range(DERIVATIVES):
            factorial = factorial * (m + 1)
            weights[m] = (up - low) * (1.0 / factorial)
            up, low = up * upper, low * lower

        for q in range(QUANTITIES):
            value = cur[q]
            operand[:, columns(q)] = stacked(value)
            integ[q] = (value.reshape(7, 8, LANES) * weights[0][None]).reshape(BASIS, LANES)

        def derivative(m, carry):
            mix(d_mat)
            weight = weights[m]

            def sink(p, value):
                operand[:, columns(p)] = stacked(value)
                integ[p] = integ[p] + (value.reshape(7, 8, LANES) * weight[None]).reshape(BASIS, LANES)

            apply_jacobians(sink)
            return carry

        lax.fori_loop(1, DERIVATIVES, derivative, 0)

        for q in range(QUANTITIES):
            operand[:, columns(q)] = stacked(integ[q])
        for q in range(0, QUANTITIES, 2):
            width = min(2, QUANTITIES - q)
            product = dot(p_mat[...], operand[:, columns(q, width)])
            for w in range(width):
                projected[q + w] = product[:, columns(w)]
        for q in range(QUANTITIES):
            for j in range(FACES):
                table[j, q * FACE_BASIS : q * FACE_BASIS + FACE_ROWS, :] = projected[
                    q, j * FACE_ROWS : (j + 1) * FACE_ROWS, :
                ]
        for j in range(FACES):
            high, low = halves(table[j])
            pair[0:PACKED, columns(j)] = high.astype(bf16)
            pair[PACKED : 2 * PACKED, columns(j)] = low.astype(bf16)

        for a in (1, 0, 2):
            product = dot(pair[:, 0 : FACES * LANES], send_hot[:, columns(2 * a, 2)])
            product = product[0:PACKED] + product[PACKED : 2 * PACKED]
            for side in range(2):
                k = 2 * a + side
                send_buf[s, k] = product[:, columns(side)]

        @pl.when(s == 0)
        def _():
            pl.semaphore_wait(barrier, arrivals)

        for k in (2, 3, 0, 1, 4, 5):

            @pl.when(sends(k))
            def _(k=k):
                copy(s, k).start()

        for i in range(0, FACES, 2):
            product = dot(pair[:, 0 : FACES * LANES], recv_hot[0 : FACES * LANES, columns(i, 2)])
            product = product[0:PACKED] + product[PACKED : 2 * PACKED]
            inner[i] = product[:, columns(0)]
            inner[i + 1] = product[:, columns(1)]

        def solve(i, blocks, solver, sink):
            for p0 in range(0, QUANTITIES, 3):
                sums = [None] * 3
                for q in range(QUANTITIES):
                    part = blocks(q).reshape(3, 8, LANES)
                    for w in range(3):
                        term = part * solver[(i * 9 + q) * 9 + p0 + w][None]
                        sums[w] = term if sums[w] is None else sums[w] + term
                for w in range(3):
                    sink(p0 + w, sums[w].reshape(FACE_ROWS, LANES))

        for i in range(FACES):
            rows = slice(i * FACE_ROWS, (i + 1) * FACE_ROWS)

            def keep(p, value, rows=rows):
                zface[p, rows, :] = value

            solve(i, lambda q, rows=rows: projected[q, rows, :], ls_b, keep)

        for q in range(QUANTITIES):
            value = own[q] + integ[q]
            own[q] = value
            operand[:, columns(q)] = stacked(value)
        mix(v_mat)

        def keep_volume(p, value):
            volume[p] = value

        apply_jacobians(keep_volume)

        for k in (4, 5, 0, 1, 2, 3):

            @pl.when(receives(k))
            def _(k=k):
                copy(s, k).wait_recv()

        for k in range(DIRECTIONS):
            high, low = halves(recv_buf[s, k])
            pair[0:PACKED, columns(k)] = high.astype(bf16)
            pair[PACKED : 2 * PACKED, columns(k)] = low.astype(bf16)
        for i in range(0, FACES, 2):
            product = dot(pair[...], recv_hot[FACES * LANES :, columns(i, 2)])
            product = product[0:PACKED] + product[PACKED : 2 * PACKED]
            total[i] = inner[i] + product[:, columns(0)]
            total[i + 1] = inner[i + 1] + product[:, columns(1)]

        for i in range(FACES):
            rows = slice(i * FACE_ROWS, (i + 1) * FACE_ROWS)
            turn = jnp.broadcast_to(orient_ref[i : i + 1, :], (8, LANES))[None]
            for q in range(QUANTITIES):
                zstack[0 : 3 * FACE_ROWS, columns(q)] = stacked(
                    total[i, q * FACE_BASIS : q * FACE_BASIS + FACE_ROWS, :]
                )
            for q in range(0, QUANTITIES, 2):
                width = min(2, QUANTITIES - q)
                product = dot(r_mat[...], zstack[0 : 3 * FACE_ROWS, columns(q, width)])
                for w in range(width):
                    parts = [
                        product[o * FACE_ROWS : (o + 1) * FACE_ROWS, columns(w)].reshape(3, 8, LANES)
                        for o in range(3)
                    ]
                    picked = jnp.where(turn == 0, parts[0], jnp.where(turn == 1, parts[1], parts[2]))
                    chosen[q + w] = picked.reshape(FACE_ROWS, LANES)

            def add(p, value, rows=rows):
                zface[p, rows, :] = zface[p, rows, :] + value

            solve(i, lambda q: chosen[q], ns_b, add)

        for p in range(QUANTITIES):
            zstack[:, columns(p)] = stacked(zface[p])
        for p in range(0, QUANTITIES, 2):
            width = min(2, QUANTITIES - p)
            product = dot(l_mat[...], zstack[:, columns(p, width)])
            for w in range(width):
                at = p + w
                done = ending[None]
                fluxes = (flux[at] + product[:, columns(w)]).reshape(7, 8, LANES)
                old = cur[at].reshape(7, 8, LANES)
                fresh = old + volume[at].reshape(7, 8, LANES) - fluxes
                cur[at] = jnp.where(done, fresh, old).reshape(BASIS, LANES)
                flux[at] = jnp.where(done, 0.0, fluxes).reshape(BASIS, LANES)
                own[at] = jnp.where(done, 0.0, own[at].reshape(7, 8, LANES)).reshape(BASIS, LANES)
        return carry

    lax.fori_loop(0, SUBSTEPS, substep, 0)

    for s in range(SUBSTEPS):
        for k in range(DIRECTIONS):

            @pl.when(sends(k))
            def _(s=s, k=k):
                copy(s, k).wait_send()

    for q in range(QUANTITIES):
        out_ref[:, q, :] = cur[q]


def local(*arrays):
    arrays = list(arrays)
    arrays[9] = arrays[9].reshape(1, LANES)
    width = QUANTITIES * LANES
    state = pltpu.VMEM((QUANTITIES, BASIS, LANES), f32)
    vmem = pltpu.VMEM
    return pl.pallas_call(
        kernel,
        out_shape=jax.ShapeDtypeStruct((BASIS, QUANTITIES, LANES), f32),
        in_specs=[pl.BlockSpec(memory_space=pltpu.VMEM)] * len(arrays),
        out_specs=pl.BlockSpec(memory_space=pltpu.VMEM),
        scratch_shapes=[
            state,
            state,
            state,
            state,
            vmem((QUANTITIES, 3 * BASIS, LANES), f32),
            state,
            vmem((3 * BASIS, width), bf16),
            vmem((QUANTITIES, FACES * FACE_ROWS, LANES), f32),
            vmem((FACES, PACKED, LANES), f32),
            vmem((2 * PACKED, DIRECTIONS * LANES), bf16),
            vmem((FACES, PACKED, LANES), f32),
            vmem((FACES, PACKED, LANES), f32),
            vmem((QUANTITIES, FACE_ROWS, LANES), f32),
            vmem((QUANTITIES, FACES * FACE_ROWS, LANES), f32),
            vmem((3 * FACES * FACE_ROWS, width), bf16),
            vmem((3 * 81, 8, LANES), f32),
            vmem((4 * 81, 8, LANES), f32),
            vmem((4 * 81, 8, LANES), f32),
            vmem((DERIVATIVES, 8, LANES), f32),
            vmem((3 * BASIS, 3 * BASIS), bf16),
            vmem((3 * BASIS, 3 * BASIS), bf16),
            vmem((FACES * FACE_ROWS, 3 * BASIS), bf16),
            vmem((BASIS, 3 * FACES * FACE_ROWS), bf16),
            vmem((3 * FACE_ROWS, 3 * FACE_ROWS), bf16),
            vmem((FACES * FACE_ROWS, 3 * BASIS), f32),
            vmem((3 * FACE_ROWS, 3 * FACE_ROWS), f32),
            vmem((FACES * LANES, DIRECTIONS * LANES), bf16),
            vmem(((FACES + DIRECTIONS) * LANES, FACES * LANES), bf16),
            vmem((SUBSTEPS, DIRECTIONS, PACKED, LANES), f32),
            vmem((SUBSTEPS, DIRECTIONS, PACKED, LANES), f32),
            pltpu.SemaphoreType.DMA((SUBSTEPS, DIRECTIONS)),
            pltpu.SemaphoreType.DMA((SUBSTEPS, DIRECTIONS)),
        ],
        compiler_params=pltpu.CompilerParams(
            collective_id=0, has_side_effects=True, vmem_limit_bytes=56 * 1024 * 1024
        ),
    )(*arrays)


def solution(mesh):
    spread = ("gx", "gy", "gz")
    return jax.shard_map(
        local,
        mesh=mesh,
        in_specs=(
            P(None, None, spread),
            P(None, None, None, spread),
            P(),
            P(),
            P(),
            P(),
            P(),
            P(None, None, None, spread),
            P(None, None, None, spread),
            P(spread),
            P(None, spread),
            P(None, spread),
            P(None, spread),
            P(None, spread),
        ),
        out_specs=P(None, None, spread),
        check_vma=False,
    )
```

```python
import jax
import jax.numpy as jnp
from jax import lax
from jax.experimental import pallas as pl
from jax.experimental.pallas import tpu as pltpu
from jax.sharding import PartitionSpec as P

BASIS = 56
QUANTITIES = 9
FACE_BASIS = 21
DERIVATIVES = 6
SUBSTEPS = 4
LANES = 128
FACES = 4
DIRECTIONS = 6
FACE_ROWS = 24
CHUNKS = 3
CHUNK_ROWS = 64
BLOCKS = ((0, 4), (4, 8), (8, 9))
MESH = pl.DeviceIdType.MESH
AXES = ("gx", "gy", "gz")

f32 = jnp.float32
bf16 = jnp.bfloat16


def halves(value):
    high = value.astype(bf16).astype(f32)
    return high, value - high


def stacked(value):
    high, low = halves(value)
    return jnp.concatenate([high, low, high], axis=0).astype(bf16)


def place(rows, columns, offsets):
    row = lax.broadcasted_iota(jnp.int32, (rows, columns), 0)
    column = lax.broadcasted_iota(jnp.int32, (rows, columns), 1)
    hit = column == row + offsets[0]
    for offset in offsets[1:]:
        hit = hit | (column == row + offset)
    return jnp.where(hit, 1.0, 0.0).astype(bf16)


def widened(matrix, columns, first, second, third, turned=False):
    high, low = halves(matrix)
    depth = matrix.shape[0 if turned else 1]
    dims = (((0 if turned else 1,), (0,)), ((), ()))
    both = place(depth, columns, (first, second))
    return lax.dot_general(
        high.astype(bf16), both, dims, preferred_element_type=f32
    ) + lax.dot_general(
        low.astype(bf16), place(depth, columns, (third,)), dims, preferred_element_type=f32
    )


def dot(left, right):
    return jnp.dot(left, right, preferred_element_type=f32)


def kernel(
    sol_ref, jac_ref, ds_ref, vs_ref, fp_ref, fl_ref, fr_ref, ls_ref, ns_ref,
    cluster_ref, neigh_ref, orient_ref, faces_ref, counts_ref, out_ref,
    own, flux, integ, mixed_0, mixed_1, volume, projected, table, pair,
    inner, total, zface, jac_b, ls_b, ns_b, weights,
    d_mat, v_mat, p_mat, l_mat, r_mat, build, build2, send_hot, recv_hot,
    send_buf, recv_buf, send_sem, recv_sem,
):
    cur = out_ref
    mixed = (mixed_0, mixed_1)
    index = [lax.axis_index(name) for name in AXES]
    count = [lax.axis_size(name) for name in AXES]
    has_lower = [index[a] > 0 for a in range(3)]
    has_higher = [index[a] < count[a] - 1 for a in range(3)]

    barrier = pltpu.get_barrier_semaphore()
    arrivals = jnp.int32(0)
    for a in range(3):
        for there, step in ((has_lower[a], -1), (has_higher[a], 1)):
            arrivals = arrivals + there.astype(jnp.int32)

            @pl.when(there)
            def _(a=a, step=step):
                pl.semaphore_signal(
                    barrier, inc=1, device_id={AXES[a]: index[a] + step}, device_id_type=MESH
                )

    for d in range(3):
        for q in range(QUANTITIES):
            for p in range(QUANTITIES):
                jac_b[(d * 9 + q) * 9 + p] = jnp.broadcast_to(jac_ref[q, p, d : d + 1, :], (8, LANES))
    d_mat[...] = widened(-ds_ref[...].reshape(3 * BASIS, BASIS), 3 * BASIS, 0, BASIS, 2 * BASIS).astype(bf16)
    for q in range(QUANTITIES):
        cur[q] = sol_ref[q]
        own[q] = jnp.zeros((BASIS, LANES), f32)
        flux[q] = jnp.zeros((BASIS, LANES), f32)
    build[...] = jnp.zeros_like(build)
    for j in range(FACES):
        build[j * FACE_ROWS : j * FACE_ROWS + FACE_BASIS, :] = widened(
            fp_ref[:, j, :], 3 * BASIS, 0, BASIS, 2 * BASIS
        )
    p_mat[...] = build[...].astype(bf16)
    slot = lax.broadcasted_iota(jnp.int32, (1, LANES), 1)
    face_row = lax.broadcasted_iota(jnp.int32, (FACES * LANES, LANES), 0)
    for k in range(DIRECTIONS):
        named = jnp.where(slot < counts_ref[:, k : k + 1], faces_ref[k : k + 1, :], -1)
        send_hot[:, k * LANES : (k + 1) * LANES] = jnp.where(face_row == named, 1.0, 0.0).astype(bf16)
    for a in range(3):
        for side in range(2):

            @pl.when(jnp.logical_not((has_lower, has_higher)[side][a]))
            def _(k=2 * a + side):
                for step in range(SUBSTEPS):
                    recv_buf[step, k] = jnp.zeros((CHUNKS, CHUNK_ROWS, LANES), f32)

    def late_constants():
        for start, rows, value in ((0, 768, 0), (768, 256, 1024), (1024, 256, 768)):
            block_row = lax.broadcasted_iota(jnp.int32, (rows, LANES), 0) + value
            for i in range(FACES):
                recv_hot[start : start + rows, i * LANES : (i + 1) * LANES] = jnp.where(
                    block_row == neigh_ref[i : i + 1, :], 1.0, 0.0
                ).astype(bf16)
        for i in range(FACES):
            for q in range(QUANTITIES):
                for p in range(QUANTITIES):
                    at = (i * 9 + q) * 9 + p
                    ls_b[at] = jnp.broadcast_to(ls_ref[q, p, i : i + 1, :], (8, LANES))
                    ns_b[at] = jnp.broadcast_to(ns_ref[q, p, i : i + 1, :], (8, LANES))
        v_mat[...] = widened(vs_ref[...].reshape(3 * BASIS, BASIS), 3 * BASIS, 0, BASIS, 2 * BASIS).astype(bf16)
        width = FACES * FACE_ROWS
        joined = jnp.zeros((BASIS, 3 * width), f32)
        for i in range(FACES):
            at = i * FACE_ROWS
            joined = joined + widened(fl_ref[:, i, :], 3 * width, at, width + at, 2 * width + at, True)
        l_mat[...] = joined.astype(bf16)
        build2[...] = jnp.zeros_like(build2)
        for o in range(3):
            build2[o * FACE_ROWS : o * FACE_ROWS + FACE_BASIS, :] = widened(
                fr_ref[o], 3 * FACE_ROWS, 0, FACE_ROWS, 2 * FACE_ROWS
            )
        r_mat[...] = build2[...].astype(bf16)
        total[...] = jnp.zeros_like(total)

    def columns(q, width=1):
        return slice(q * LANES, (q + width) * LANES)

    def tall(value, scale):
        shape = value.shape
        return (value.reshape(shape[0] // 8, 8, LANES) * scale[None]).reshape(shape)

    def beside(pieces):
        return pieces[0] if len(pieces) == 1 else jnp.concatenate(pieces, axis=1)

    def mix(matrix, slot, first, pieces):
        for q in range(0, len(pieces), 2):
            some = pieces[q : q + 2]
            product = dot(matrix[...], beside(some))
            for w in range(len(some)):
                mixed[slot][first + q + w] = product[:, columns(w)]

    def apply_jacobians(slot, p0, wide):
        sums = [None] * wide
        for q in range(QUANTITIES):
            for d in range(3):
                part = mixed[slot][q, d * BASIS : (d + 1) * BASIS, :]
                for w in range(wide):
                    term = tall(part, jac_b[(d * 9 + q) * 9 + p0 + w])
                    sums[w] = term if sums[w] is None else sums[w] + term
        return sums

    def copy(s, k):
        a, side = k // 2, k % 2
        return pltpu.make_async_remote_copy(
            src_ref=send_buf.at[s, k],
            dst_ref=recv_buf.at[s, k],
            send_sem=send_sem.at[s, k],
            recv_sem=recv_sem.at[s, k],
            device_id={AXES[a]: index[a] + (1, -1)[side]},
            device_id_type=MESH,
        )

    def sends(k):
        return (has_higher, has_lower)[k % 2][k // 2]

    def receives(k):
        return (has_lower, has_higher)[k % 2][k // 2]

    def combined(product, chunk):
        at = 2 * CHUNK_ROWS * chunk
        return product[at : at + CHUNK_ROWS] + product[at + CHUNK_ROWS : at + 2 * CHUNK_ROWS]

    def fill_pair(chunk, column, value):
        high, low = halves(value)
        at = 2 * CHUNK_ROWS * chunk
        pair[at : at + CHUNK_ROWS, columns(column)] = high.astype(bf16)
        pair[at + CHUNK_ROWS : at + 2 * CHUNK_ROWS, columns(column)] = low.astype(bf16)

    period = jnp.left_shift(jnp.ones((8, LANES), jnp.int32), jnp.broadcast_to(cluster_ref[...], (8, LANES)))

    def substep(s, carry):
        offset = (s & (period - 1)).astype(f32)
        ending = ((s + 1) & (period - 1)) == 0
        upper, lower = (offset + 1.0) * 0.25, offset * 0.25
        up, low, factorial = upper, lower, 1.0
        for m in range(DERIVATIVES):
            factorial = factorial * (m + 1)
            weights[m] = (up - low) * (1.0 / factorial)
            up, low = up * upper, low * lower

        held = {}
        for first, last in BLOCKS:
            pieces = []
            for q in range(first, last):
                value = cur[q]
                pieces.append(stacked(value))
                held[q] = tall(value, weights[0])
            mix(d_mat, 0, first, pieces)
        for m in range(1, DERIVATIVES - 1):
            here, there = (m - 1) % 2, m % 2
            for first, last in BLOCKS:
                fresh = apply_jacobians(here, first, last - first)
                pieces = []
                for w, value in enumerate(fresh):
                    pieces.append(stacked(value))
                    held[first + w] = held[first + w] + tall(value, weights[m])
                mix(d_mat, there, first, pieces)
        here = (DERIVATIVES - 2) % 2
        for chunk in range(CHUNKS):
            first = 3 * chunk
            pieces = []
            fresh = apply_jacobians(here, first, 3)
            for w, value in enumerate(fresh):
                value = held[first + w] + tall(value, weights[DERIVATIVES - 1])
                integ[first + w] = value
                pieces.append(stacked(value))
            for q, width in ((0, 2), (2, 1)):
                product = dot(p_mat[...], beside(pieces[q : q + width]))
                for w in range(width):
                    at = q + w
                    projected[first + at] = product[:, columns(w)]
                    for j in range(FACES):
                        table[chunk, j, at * FACE_BASIS : at * FACE_BASIS + FACE_ROWS, :] = product[
                            j * FACE_ROWS : (j + 1) * FACE_ROWS, columns(w)
                        ]
            for j in range(FACES):
                fill_pair(chunk, j, table[chunk, j, 0:CHUNK_ROWS, :])

        @pl.when(s == 0)
        def _():
            pl.semaphore_wait(barrier, arrivals)

        for a in (1, 2, 0):
            product = dot(pair[:, 0 : FACES * LANES], send_hot[:, columns(2 * a, 2)])
            for chunk in range(CHUNKS):
                part = combined(product, chunk)
                for side in range(2):
                    send_buf[s, 2 * a + side, chunk] = part[:, columns(side)]
            for k in (2 * a, 2 * a + 1):

                @pl.when(sends(k))
                def _(k=k):
                    copy(s, k).start()

        @pl.when(s == 0)
        def _():
            late_constants()

        pieces = []
        for q in range(QUANTITIES):
            value = own[q] + integ[q]
            own[q] = value
            pieces.append(stacked(value))
        mix(v_mat, 0, 0, pieces)
        for first in range(0, QUANTITIES, 3):
            for w, value in enumerate(apply_jacobians(0, first, 3)):
                volume[first + w] = value
        for i in range(FACES):
            rows = slice(i * FACE_ROWS, (i + 1) * FACE_ROWS)
            for p0 in range(0, QUANTITIES, 3):
                sums = [None] * 3
                for q in range(QUANTITIES):
                    part = projected[q, rows, :]
                    for w in range(3):
                        term = tall(part, ls_b[(i * 9 + q) * 9 + p0 + w])
                        sums[w] = term if sums[w] is None else sums[w] + term
                for w in range(3):
                    zface[p0 + w, rows, :] = sums[w]

        for k in (4, 5, 0, 1):

            @pl.when(receives(k))
            def _(k=k):
                copy(s, k).wait_recv()

        for at, k in enumerate((0, 1, 4, 5)):
            for chunk in range(CHUNKS):
                fill_pair(chunk, FACES + at, recv_buf[s, k, chunk])
        early = 8 * LANES
        for i in range(0, FACES, 2):
            product = dot(pair[:, 0:early], recv_hot[0:early, columns(i, 2)])
            for chunk in range(CHUNKS):
                part = combined(product, chunk)
                for w in range(2):
                    inner[chunk, i + w] = part[:, columns(w)]

        for k in (2, 3):

            @pl.when(receives(k))
            def _(k=k):
                copy(s, k).wait_recv()

        for chunk in range(CHUNKS):
            for k in (2, 3):
                fill_pair(chunk, 6 + k, recv_buf[s, k, chunk])
        for i in range(0, FACES, 2):
            product = dot(pair[:, early:], recv_hot[early:, columns(i, 2)])
            for chunk in range(CHUNKS):
                part = combined(product, chunk)
                for w in range(2):
                    total[i + w, chunk, 0:CHUNK_ROWS, :] = inner[chunk, i + w] + part[:, columns(w)]
        for i in range(FACES):
            rows = slice(i * FACE_ROWS, (i + 1) * FACE_ROWS)
            turn = jnp.broadcast_to(orient_ref[i : i + 1, :], (8, LANES))[None]
            pieces = []
            for q in range(QUANTITIES):
                at = (q % 3) * FACE_BASIS
                pieces.append(stacked(total[i, q // 3, at : at + FACE_ROWS, :]))
            picked = []
            for q0 in range(0, QUANTITIES, 2):
                wide = min(2, QUANTITIES - q0)
                product = dot(r_mat[...], beside(pieces[q0 : q0 + wide]))
                for w in range(wide):
                    parts = [
                        product[o * FACE_ROWS : (o + 1) * FACE_ROWS, columns(w)].reshape(3, 8, LANES)
                        for o in range(3)
                    ]
                    value = jnp.where(turn == 0, parts[0], jnp.where(turn == 1, parts[1], parts[2]))
                    picked.append(value.reshape(FACE_ROWS, LANES))
            for p0 in range(0, QUANTITIES, 3):
                sums = [zface[p0 + w, rows, :] for w in range(3)]
                for q in range(QUANTITIES):
                    part = picked[q]
                    for w in range(3):
                        sums[w] = sums[w] + tall(part, ns_b[(i * 9 + q) * 9 + p0 + w])
                for w in range(3):
                    zface[p0 + w, rows, :] = sums[w]

        for p in range(0, QUANTITIES, 2):
            width = min(2, QUANTITIES - p)
            product = dot(l_mat[...], beside([stacked(zface[p + w]) for w in range(width)]))
            for w in range(width):
                at = p + w
                done = ending[None]
                fluxes = (flux[at] + product[:, columns(w)]).reshape(7, 8, LANES)
                old = cur[at].reshape(7, 8, LANES)
                fresh = old + volume[at].reshape(7, 8, LANES) - fluxes
                cur[at] = jnp.where(done, fresh, old).reshape(BASIS, LANES)
                flux[at] = jnp.where(done, 0.0, fluxes).reshape(BASIS, LANES)
                own[at] = jnp.where(done, 0.0, own[at].reshape(7, 8, LANES)).reshape(BASIS, LANES)
        return carry

    lax.fori_loop(0, SUBSTEPS, substep, 0)

    for s in range(SUBSTEPS):
        for k in range(DIRECTIONS):

            @pl.when(sends(k))
            def _(s=s, k=k):
                copy(s, k).wait_send()


def local(*arrays):
    arrays = list(arrays)
    arrays[0] = arrays[0].transpose(1, 0, 2)
    for at in (1, 7, 8):
        arrays[at] = arrays[at].transpose(1, 2, 0, 3)
    arrays[4] = arrays[4].transpose(1, 0, 2)
    arrays[5] = arrays[5].transpose(2, 0, 1)
    arrays[9] = arrays[9].reshape(1, LANES)
    arrays[13] = arrays[13].reshape(1, DIRECTIONS)
    state = pltpu.VMEM((QUANTITIES, BASIS, LANES), f32)
    vmem = pltpu.VMEM
    advanced = pl.pallas_call(
        kernel,
        out_shape=jax.ShapeDtypeStruct((QUANTITIES, BASIS, LANES), f32),
        in_specs=[pl.BlockSpec(memory_space=pltpu.VMEM)] * len(arrays),
        out_specs=pl.BlockSpec(memory_space=pltpu.VMEM),
        scratch_shapes=[
            state,
            state,
            state,
            vmem((QUANTITIES, 3 * BASIS, LANES), f32),
            vmem((QUANTITIES, 3 * BASIS, LANES), f32),
            state,
            vmem((QUANTITIES, FACES * FACE_ROWS, LANES), f32),
            vmem((CHUNKS, FACES, 72, LANES), f32),
            vmem((CHUNKS * 2 * CHUNK_ROWS, (FACES + DIRECTIONS) * LANES), bf16),
            vmem((CHUNKS, FACES, CHUNK_ROWS, LANES), f32),
            vmem((FACES, CHUNKS, 72, LANES), f32),
            vmem((QUANTITIES, FACES * FACE_ROWS, LANES), f32),
            vmem((3 * 81, 8, LANES), f32),
            vmem((4 * 81, 8, LANES), f32),
            vmem((4 * 81, 8, LANES), f32),
            vmem((DERIVATIVES, 8, LANES), f32),
            vmem((3 * BASIS, 3 * BASIS), bf16),
            vmem((3 * BASIS, 3 * BASIS), bf16),
            vmem((FACES * FACE_ROWS, 3 * BASIS), bf16),
            vmem((BASIS, 3 * FACES * FACE_ROWS), bf16),
            vmem((3 * FACE_ROWS, 3 * FACE_ROWS), bf16),
            vmem((FACES * FACE_ROWS, 3 * BASIS), f32),
            vmem((3 * FACE_ROWS, 3 * FACE_ROWS), f32),
            vmem((FACES * LANES, DIRECTIONS * LANES), bf16),
            vmem(((FACES + DIRECTIONS) * LANES, FACES * LANES), bf16),
            vmem((SUBSTEPS, DIRECTIONS, CHUNKS, CHUNK_ROWS, LANES), f32),
            vmem((SUBSTEPS, DIRECTIONS, CHUNKS, CHUNK_ROWS, LANES), f32),
            pltpu.SemaphoreType.DMA((SUBSTEPS, DIRECTIONS)),
            pltpu.SemaphoreType.DMA((SUBSTEPS, DIRECTIONS)),
        ],
        compiler_params=pltpu.CompilerParams(
            collective_id=0, has_side_effects=True, vmem_limit_bytes=56 * 1024 * 1024
        ),
    )(*arrays)
    return advanced.transpose(1, 0, 2)


def solution(mesh):
    spread = ("gx", "gy", "gz")
    return jax.shard_map(
        local,
        mesh=mesh,
        in_specs=(
            P(None, None, spread),
            P(None, None, None, spread),
            P(),
            P(),
            P(),
            P(),
            P(),
            P(None, None, None, spread),
            P(None, None, None, spread),
            P(spread),
            P(None, spread),
            P(None, spread),
            P(None, spread),
            P(None, spread),
        ),
        out_specs=P(None, None, spread),
        check_vma=False,
    )
```

```python
import jax
import jax.numpy as jnp
from jax import lax
from jax.experimental import pallas as pl
from jax.experimental.pallas import tpu as pltpu
from jax.sharding import PartitionSpec as P

BASIS = 56
QUANTITIES = 9
FACE_BASIS = 21
DERIVATIVES = 6
SUBSTEPS = 4
LANES = 128
FACES = 4
DIRECTIONS = 6
FACE_ROWS = 24
CHUNKS = 3
CHUNK_ROWS = 64
BLOCKS = ((0, 4), (4, 8), (8, 9))
MESH = pl.DeviceIdType.MESH
AXES = ("gx", "gy", "gz")

f32 = jnp.float32
bf16 = jnp.bfloat16


def halves(value):
    high = value.astype(bf16).astype(f32)
    return high, value - high


def stacked(value):
    high, low = halves(value)
    return jnp.concatenate([high, low, high], axis=0).astype(bf16)


def place(rows, columns, offsets):
    row = lax.broadcasted_iota(jnp.int32, (rows, columns), 0)
    column = lax.broadcasted_iota(jnp.int32, (rows, columns), 1)
    hit = column == row + offsets[0]
    for offset in offsets[1:]:
        hit = hit | (column == row + offset)
    return jnp.where(hit, 1.0, 0.0).astype(bf16)


def widened(matrix, columns, first, second, third, turned=False):
    high, low = halves(matrix)
    depth = matrix.shape[0 if turned else 1]
    dims = (((0 if turned else 1,), (0,)), ((), ()))
    both = place(depth, columns, (first, second))
    return lax.dot_general(
        high.astype(bf16), both, dims, preferred_element_type=f32
    ) + lax.dot_general(
        low.astype(bf16), place(depth, columns, (third,)), dims, preferred_element_type=f32
    )


def dot(left, right):
    return jnp.dot(left, right, preferred_element_type=f32)


def kernel(
    sol_hbm, jac_hbm, ds_ref, vs_ref, fp_ref, fl_ref, fr_ref, ls_hbm, ns_hbm,
    cluster_ref, neigh_ref, orient_ref, faces_ref, counts_ref, out_ref,
    own, flux, integ, mixed_0, mixed_1, volume, projected, table, pair,
    inner, total, zface, jac_b, ls_b, ns_b, weights,
    d_mat, v_mat, p_mat, l_mat, r_mat, build, build2, send_hot, recv_hot,
    send_buf, recv_buf, send_sem, recv_sem, jac_ref, ls_ref, ns_ref, load_sem,
):
    cur = out_ref
    loads = [
        pltpu.make_async_copy(source, target, load_sem.at[at])
        for at, (source, target) in enumerate(
            ((jac_hbm, jac_ref), (sol_hbm, cur), (ls_hbm, ls_ref), (ns_hbm, ns_ref))
        )
    ]
    for load in loads:
        load.start()
    mixed = (mixed_0, mixed_1)
    index = [lax.axis_index(name) for name in AXES]
    count = [lax.axis_size(name) for name in AXES]
    has_lower = [index[a] > 0 for a in range(3)]
    has_higher = [index[a] < count[a] - 1 for a in range(3)]

    barrier = pltpu.get_barrier_semaphore()
    arrivals = jnp.int32(0)
    for a in range(3):
        for there, step in ((has_lower[a], -1), (has_higher[a], 1)):
            arrivals = arrivals + there.astype(jnp.int32)

            @pl.when(there)
            def _(a=a, step=step):
                pl.semaphore_signal(
                    barrier, inc=1, device_id={AXES[a]: index[a] + step}, device_id_type=MESH
                )

    loads[0].wait()
    for d in range(3):
        for q in range(QUANTITIES):
            for p in range(QUANTITIES):
                jac_b[(d * 9 + q) * 9 + p] = jnp.broadcast_to(jac_ref[q, p, d : d + 1, :], (8, LANES))
    d_mat[...] = widened(-ds_ref[...].reshape(3 * BASIS, BASIS), 3 * BASIS, 0, BASIS, 2 * BASIS).astype(bf16)
    for q in range(QUANTITIES):
        own[q] = jnp.zeros((BASIS, LANES), f32)
        flux[q] = jnp.zeros((BASIS, LANES), f32)
    build[...] = jnp.zeros_like(build)
    for j in range(FACES):
        build[j * FACE_ROWS : j * FACE_ROWS + FACE_BASIS, :] = widened(
            fp_ref[:, j, :], 3 * BASIS, 0, BASIS, 2 * BASIS
        )
    p_mat[...] = build[...].astype(bf16)
    slot = lax.broadcasted_iota(jnp.int32, (1, LANES), 1)
    face_row = lax.broadcasted_iota(jnp.int32, (FACES * LANES, LANES), 0)
    for k in range(DIRECTIONS):
        named = jnp.where(slot < counts_ref[:, k : k + 1], faces_ref[k : k + 1, :], -1)
        send_hot[:, k * LANES : (k + 1) * LANES] = jnp.where(face_row == named, 1.0, 0.0).astype(bf16)
    for a in range(3):
        for side in range(2):

            @pl.when(jnp.logical_not((has_lower, has_higher)[side][a]))
            def _(k=2 * a + side):
                for step in range(SUBSTEPS):
                    recv_buf[step, k] = jnp.zeros((CHUNKS, CHUNK_ROWS, LANES), f32)

    def late_constants():
        loads[2].wait()
        loads[3].wait()
        for start, rows, value in ((0, 768, 0), (768, 256, 1024), (1024, 256, 768)):
            block_row = lax.broadcasted_iota(jnp.int32, (rows, LANES), 0) + value
            for i in range(FACES):
                recv_hot[start : start + rows, i * LANES : (i + 1) * LANES] = jnp.where(
                    block_row == neigh_ref[i : i + 1, :], 1.0, 0.0
                ).astype(bf16)
        for i in range(FACES):
            for q in range(QUANTITIES):
                for p in range(QUANTITIES):
                    at = (i * 9 + q) * 9 + p
                    ls_b[at] = jnp.broadcast_to(ls_ref[q, p, i : i + 1, :], (8, LANES))
                    ns_b[at] = jnp.broadcast_to(ns_ref[q, p, i : i + 1, :], (8, LANES))
        v_mat[...] = widened(vs_ref[...].reshape(3 * BASIS, BASIS), 3 * BASIS, 0, BASIS, 2 * BASIS).astype(bf16)
        width = FACES * FACE_ROWS
        joined = jnp.zeros((BASIS, 3 * width), f32)
        for i in range(FACES):
            at = i * FACE_ROWS
            joined = joined + widened(fl_ref[:, i, :], 3 * width, at, width + at, 2 * width + at, True)
        l_mat[...] = joined.astype(bf16)
        build2[...] = jnp.zeros_like(build2)
        for o in range(3):
            build2[o * FACE_ROWS : o * FACE_ROWS + FACE_BASIS, :] = widened(
                fr_ref[o], 3 * FACE_ROWS, 0, FACE_ROWS, 2 * FACE_ROWS
            )
        r_mat[...] = build2[...].astype(bf16)
        total[...] = jnp.zeros_like(total)

    def columns(q, width=1):
        return slice(q * LANES, (q + width) * LANES)

    def tall(value, scale):
        shape = value.shape
        return (value.reshape(shape[0] // 8, 8, LANES) * scale[None]).reshape(shape)

    def beside(pieces):
        return pieces[0] if len(pieces) == 1 else jnp.concatenate(pieces, axis=1)

    def mix(matrix, slot, first, pieces):
        for q in range(0, len(pieces), 2):
            some = pieces[q : q + 2]
            product = dot(matrix[...], beside(some))
            for w in range(len(some)):
                mixed[slot][first + q + w] = product[:, columns(w)]

    def apply_jacobians(slot, p0, wide):
        sums = [None] * wide
        for q in range(QUANTITIES):
            for d in range(3):
                part = mixed[slot][q, d * BASIS : (d + 1) * BASIS, :]
                for w in range(wide):
                    term = tall(part, jac_b[(d * 9 + q) * 9 + p0 + w])
                    sums[w] = term if sums[w] is None else sums[w] + term
        return sums

    def copy(s, k):
        a, side = k // 2, k % 2
        return pltpu.make_async_remote_copy(
            src_ref=send_buf.at[s, k],
            dst_ref=recv_buf.at[s, k],
            send_sem=send_sem.at[s, k],
            recv_sem=recv_sem.at[s, k],
            device_id={AXES[a]: index[a] + (1, -1)[side]},
            device_id_type=MESH,
        )

    def sends(k):
        return (has_higher, has_lower)[k % 2][k // 2]

    def receives(k):
        return (has_lower, has_higher)[k % 2][k // 2]

    def combined(product, chunk):
        at = 2 * CHUNK_ROWS * chunk
        return product[at : at + CHUNK_ROWS] + product[at + CHUNK_ROWS : at + 2 * CHUNK_ROWS]

    def fill_pair(chunk, column, value):
        high, low = halves(value)
        at = 2 * CHUNK_ROWS * chunk
        pair[at : at + CHUNK_ROWS, columns(column)] = high.astype(bf16)
        pair[at + CHUNK_ROWS : at + 2 * CHUNK_ROWS, columns(column)] = low.astype(bf16)

    period = jnp.left_shift(jnp.ones((8, LANES), jnp.int32), jnp.broadcast_to(cluster_ref[...], (8, LANES)))

    loads[1].wait()

    def substep(s, carry):
        offset = (s & (period - 1)).astype(f32)
        ending = ((s + 1) & (period - 1)) == 0
        upper, lower = (offset + 1.0) * 0.25, offset * 0.25
        up, low, factorial = upper, lower, 1.0
        for m in range(DERIVATIVES):
            factorial = factorial * (m + 1)
            weights[m] = (up - low) * (1.0 / factorial)
            up, low = up * upper, low * lower

        held = {}
        for first, last in BLOCKS:
            pieces = []
            for q in range(first, last):
                value = cur[q]
                pieces.append(stacked(value))
                held[q] = tall(value, weights[0])
            mix(d_mat, 0, first, pieces)
        for m in range(1, DERIVATIVES - 1):
            here, there = (m - 1) % 2, m % 2
            for first, last in BLOCKS:
                fresh = apply_jacobians(here, first, last - first)
                pieces = []
                for w, value in enumerate(fresh):
                    pieces.append(stacked(value))
                    held[first + w] = held[first + w] + tall(value, weights[m])
                mix(d_mat, there, first, pieces)
        here = (DERIVATIVES - 2) % 2
        for chunk in range(CHUNKS):
            first = 3 * chunk
            pieces = []
            fresh = apply_jacobians(here, first, 3)
            for w, value in enumerate(fresh):
                value = held[first + w] + tall(value, weights[DERIVATIVES - 1])
                integ[first + w] = value
                pieces.append(stacked(value))
            for q, width in ((0, 2), (2, 1)):
                product = dot(p_mat[...], beside(pieces[q : q + width]))
                for w in range(width):
                    at = q + w
                    projected[first + at] = product[:, columns(w)]
                    for j in range(FACES):
                        table[chunk, j, at * FACE_BASIS : at * FACE_BASIS + FACE_ROWS, :] = product[
                            j * FACE_ROWS : (j + 1) * FACE_ROWS, columns(w)
                        ]
            for j in range(FACES):
                fill_pair(chunk, j, table[chunk, j, 0:CHUNK_ROWS, :])

        @pl.when(s == 0)
        def _():
            pl.semaphore_wait(barrier, arrivals)

        for a in (1, 2, 0):
            product = dot(pair[:, 0 : FACES * LANES], send_hot[:, columns(2 * a, 2)])
            for chunk in range(CHUNKS):
                part = combined(product, chunk)
                for side in range(2):
                    send_buf[s, 2 * a + side, chunk] = part[:, columns(side)]
            for k in (2 * a, 2 * a + 1):

                @pl.when(sends(k))
                def _(k=k):
                    copy(s, k).start()

        @pl.when(s == 0)
        def _():
            late_constants()

        pieces = []
        for q in range(QUANTITIES):
            value = own[q] + integ[q]
            own[q] = jnp.where(ending[None], 0.0, value.reshape(7, 8, LANES)).reshape(BASIS, LANES)
            pieces.append(stacked(value))
        mix(v_mat, 0, 0, pieces)
        for first in range(0, QUANTITIES, 3):
            for w, value in enumerate(apply_jacobians(0, first, 3)):
                volume[first + w] = value
        for i in range(FACES):
            rows = slice(i * FACE_ROWS, (i + 1) * FACE_ROWS)
            for p0 in range(0, QUANTITIES, 3):
                sums = [None] * 3
                for q in range(QUANTITIES):
                    part = projected[q, rows, :]
                    for w in range(3):
                        term = tall(part, ls_b[(i * 9 + q) * 9 + p0 + w])
                        sums[w] = term if sums[w] is None else sums[w] + term
                for w in range(3):
                    zface[p0 + w, rows, :] = sums[w]

        for k in (4, 5, 0, 1):

            @pl.when(receives(k))
            def _(k=k):
                copy(s, k).wait_recv()

        for at, k in enumerate((0, 1, 4, 5)):
            for chunk in range(CHUNKS):
                fill_pair(chunk, FACES + at, recv_buf[s, k, chunk])
        early = 8 * LANES
        for i in range(0, FACES, 2):
            product = dot(pair[:, 0:early], recv_hot[0:early, columns(i, 2)])
            for chunk in range(CHUNKS):
                part = combined(product, chunk)
                for w in range(2):
                    inner[chunk, i + w] = part[:, columns(w)]

        for k in (2, 3):

            @pl.when(receives(k))
            def _(k=k):
                copy(s, k).wait_recv()

        for chunk in range(CHUNKS):
            for k in (2, 3):
                fill_pair(chunk, 6 + k, recv_buf[s, k, chunk])
        for i in range(0, FACES, 2):
            product = dot(pair[:, early:], recv_hot[early:, columns(i, 2)])
            for chunk in range(CHUNKS):
                part = combined(product, chunk)
                for w in range(2):
                    total[i + w, chunk, 0:CHUNK_ROWS, :] = inner[chunk, i + w] + part[:, columns(w)]
        for i in range(FACES):
            rows = slice(i * FACE_ROWS, (i + 1) * FACE_ROWS)
            turn = jnp.broadcast_to(orient_ref[i : i + 1, :], (8, LANES))[None]
            pieces = []
            for q in range(QUANTITIES):
                at = (q % 3) * FACE_BASIS
                pieces.append(stacked(total[i, q // 3, at : at + FACE_ROWS, :]))
            picked = []
            for q0 in range(0, QUANTITIES, 2):
                wide = min(2, QUANTITIES - q0)
                product = dot(r_mat[...], beside(pieces[q0 : q0 + wide]))
                for w in range(wide):
                    parts = [
                        product[o * FACE_ROWS : (o + 1) * FACE_ROWS, columns(w)].reshape(3, 8, LANES)
                        for o in range(3)
                    ]
                    value = jnp.where(turn == 0, parts[0], jnp.where(turn == 1, parts[1], parts[2]))
                    picked.append(value.reshape(FACE_ROWS, LANES))
            for p0 in range(0, QUANTITIES, 3):
                sums = [zface[p0 + w, rows, :] for w in range(3)]
                for q in range(QUANTITIES):
                    part = picked[q]
                    for w in range(3):
                        sums[w] = sums[w] + tall(part, ns_b[(i * 9 + q) * 9 + p0 + w])
                for w in range(3):
                    zface[p0 + w, rows, :] = sums[w]

        for p in range(0, QUANTITIES, 2):
            width = min(2, QUANTITIES - p)
            product = dot(l_mat[...], beside([stacked(zface[p + w]) for w in range(width)]))
            for w in range(width):
                at = p + w
                done = ending[None]
                fluxes = (flux[at] + product[:, columns(w)]).reshape(7, 8, LANES)
                old = cur[at].reshape(7, 8, LANES)
                fresh = old + volume[at].reshape(7, 8, LANES) - fluxes
                cur[at] = jnp.where(done, fresh, old).reshape(BASIS, LANES)
                flux[at] = jnp.where(done, 0.0, fluxes).reshape(BASIS, LANES)
        return carry

    lax.fori_loop(0, SUBSTEPS, substep, 0)

    for s in range(SUBSTEPS):
        for k in range(DIRECTIONS):

            @pl.when(sends(k))
            def _(s=s, k=k):
                copy(s, k).wait_send()


def local(*arrays):
    arrays = list(arrays)
    arrays[0] = arrays[0].transpose(1, 0, 2)
    for at in (1, 7, 8):
        arrays[at] = arrays[at].transpose(1, 2, 0, 3)
    arrays[4] = arrays[4].transpose(1, 0, 2)
    arrays[5] = arrays[5].transpose(2, 0, 1)
    arrays[9] = arrays[9].reshape(1, LANES)
    arrays[13] = arrays[13].reshape(1, DIRECTIONS)
    state = pltpu.VMEM((QUANTITIES, BASIS, LANES), f32)
    vmem = pltpu.VMEM
    advanced = pl.pallas_call(
        kernel,
        out_shape=jax.ShapeDtypeStruct((QUANTITIES, BASIS, LANES), f32),
        in_specs=[
            pl.BlockSpec(memory_space=pl.ANY if at in (0, 1, 7, 8) else pltpu.VMEM)
            for at in range(len(arrays))
        ],
        out_specs=pl.BlockSpec(memory_space=pltpu.VMEM),
        scratch_shapes=[
            state,
            state,
            state,
            vmem((QUANTITIES, 3 * BASIS, LANES), f32),
            vmem((QUANTITIES, 3 * BASIS, LANES), f32),
            state,
            vmem((QUANTITIES, FACES * FACE_ROWS, LANES), f32),
            vmem((CHUNKS, FACES, 72, LANES), f32),
            vmem((CHUNKS * 2 * CHUNK_ROWS, (FACES + DIRECTIONS) * LANES), bf16),
            vmem((CHUNKS, FACES, CHUNK_ROWS, LANES), f32),
            vmem((FACES, CHUNKS, 72, LANES), f32),
            vmem((QUANTITIES, FACES * FACE_ROWS, LANES), f32),
            vmem((3 * 81, 8, LANES), f32),
            vmem((4 * 81, 8, LANES), f32),
            vmem((4 * 81, 8, LANES), f32),
            vmem((DERIVATIVES, 8, LANES), f32),
            vmem((3 * BASIS, 3 * BASIS), bf16),
            vmem((3 * BASIS, 3 * BASIS), bf16),
            vmem((FACES * FACE_ROWS, 3 * BASIS), bf16),
            vmem((BASIS, 3 * FACES * FACE_ROWS), bf16),
            vmem((3 * FACE_ROWS, 3 * FACE_ROWS), bf16),
            vmem((FACES * FACE_ROWS, 3 * BASIS), f32),
            vmem((3 * FACE_ROWS, 3 * FACE_ROWS), f32),
            vmem((FACES * LANES, DIRECTIONS * LANES), bf16),
            vmem(((FACES + DIRECTIONS) * LANES, FACES * LANES), bf16),
            vmem((SUBSTEPS, DIRECTIONS, CHUNKS, CHUNK_ROWS, LANES), f32),
            vmem((SUBSTEPS, DIRECTIONS, CHUNKS, CHUNK_ROWS, LANES), f32),
            pltpu.SemaphoreType.DMA((SUBSTEPS, DIRECTIONS)),
            pltpu.SemaphoreType.DMA((SUBSTEPS, DIRECTIONS)),
            vmem((QUANTITIES, QUANTITIES, 3, LANES), f32),
            vmem((QUANTITIES, QUANTITIES, FACES, LANES), f32),
            vmem((QUANTITIES, QUANTITIES, FACES, LANES), f32),
            pltpu.SemaphoreType.DMA((4,)),
        ],
        compiler_params=pltpu.CompilerParams(
            collective_id=0, has_side_effects=True, vmem_limit_bytes=56 * 1024 * 1024
        ),
    )(*arrays)
    return advanced.transpose(1, 0, 2)


def solution(mesh):
    spread = ("gx", "gy", "gz")
    return jax.shard_map(
        local,
        mesh=mesh,
        in_specs=(
            P(None, None, spread),
            P(None, None, None, spread),
            P(),
            P(),
            P(),
            P(),
            P(),
            P(None, None, None, spread),
            P(None, None, None, spread),
            P(spread),
            P(None, spread),
            P(None, spread),
            P(None, spread),
            P(None, spread),
        ),
        out_specs=P(None, None, spread),
        check_vma=False,
    )
```
